32 devices in a mesh: tp: 4 (over x, core), client: 4 (over z), region: 2 (over y).
Axes of the slice: x: 2, y: 2, z: 4, core: 2. Of those that a mesh axis runs over, the one named last changes fastest.
Arguments:
- hidden_in: bfloat16 [8, 2, 128, 1792], P(('client', 'region'), None, None, 'tp'), may hold values from -6 to 6
- target: bfloat16 [8, 2, 128, 1792], P(('client', 'region'), None, None, 'tp'), may hold values from -38 to 38, as said below
- up_weight: bfloat16 [1792, 7168], P(None, 'tp'), may hold values from -1 to 1
- down_weight: bfloat16 [7168, 1792], P('tp'), may hold values from -0.0625 to 0.0625
- noise_up: float32 [1792, 7168], P(('client', 'region'), 'tp'), may hold values from -6 to 6
- noise_down: float32 [7168, 1792], P('tp', ('client', 'region')), may hold values from -6 to 6
Outputs:
- new_up: float32 [1792, 7168], P(('client', 'region'), 'tp')
- new_down: float32 [7168, 1792], P('tp', ('client', 'region'))
The draws below stay inside these ranges and needn't reach their ends.
Inputs may be any that keep to these rules, and one draw needn't show every extreme that they name: `target`: targets of every client and step.
All inputs are finite; a program needn't handle non-finite values.
Results may differ from the reference program's by a relative error of at most 0.014.
Values may be sent and summed in bfloat16 or wider, within the bound.
A program may use at most 128 MiB of HBM per device.

```python
import math
import jax
import jax.numpy as jnp
from jax import lax

D = 1792
F = 7168
TOK = 128
STEPS = 2
CLIENTS = 8
N_CLIENT = 4
N_REGION = 2


def shared_states(key):
    first = jax.random.fold_in(key, 0)
    shape = (CLIENTS, STEPS, TOK, D)
    normal_part = jax.random.truncated_normal(first, -6.0, 6.0, shape, jnp.float32)
    return normal_part


def draw_hidden_in(key, part):
    states = shared_states(key)
    return states.astype(jnp.bfloat16)


def draw_target(key, part):
    states = shared_states(key)
    key = jax.random.fold_in(key, 11)
    key_order, key_jitter, key_noise = jax.random.split(key, 3)
    order = jax.random.permutation(key_order, CLIENTS).astype(jnp.float32)
    jitter = jax.random.uniform(key_jitter, (CLIENTS,), jnp.float32)
    spread = (order + jitter) / CLIENTS
    lowest = 0.03
    ratio = math.log(8.0 / lowest)
    client_scale = lowest * jnp.exp(spread * ratio)
    noise = jax.random.truncated_normal(key_noise, -4.0, 4.0, (CLIENTS, STEPS, TOK, D), jnp.float32)
    goals = states + client_scale[:, None, None, None] * noise
    return goals.astype(jnp.bfloat16)


def draw_up_weight(key, part):
    key = jax.random.fold_in(key, 23)
    deviation = 0.2 / math.sqrt(D)
    values = deviation * jax.random.truncated_normal(key, -4.0, 4.0, (D, F), jnp.float32)
    return values.astype(jnp.bfloat16)


def levels(own_key, extent, cuts, smallest, largest):
    def one(axis_at, parts):
        heights = jax.random.uniform(jax.random.fold_in(jax.random.fold_in(own_key, 6), axis_at), (parts,), jnp.float32, smallest / len(cuts), largest / len(cuts))
        return jnp.repeat(jnp.exp(heights), extent[axis_at] // parts).reshape((-1,) + (1,) * (len(extent) - axis_at - 1))

    loudness = one(*cuts[0])
    for cut in cuts[1:]:
        loudness = loudness * one(*cut)
    return loudness


def scatter_about(own_key, extent, scale, limit, cuts=(), held_as=jnp.bfloat16):
    drawn = jax.random.normal(own_key, extent, jnp.float32) * scale
    if len(cuts) > 0:
        drawn = levels(own_key, extent, cuts, -0.22, 0.18) * drawn
    return jnp.clip(drawn, min=-limit, max=limit).astype(held_as)


def setup_inputs(seed: int = 0) -> dict:
    key_of = jax.random.split(jax.random.key(seed), 7)
    hidden_in = draw_hidden_in(jax.random.fold_in(key_of[6], 71), 0)
    target = draw_target(jax.random.fold_in(key_of[6], 71), 0)
    up_weight = draw_up_weight(jax.random.fold_in(key_of[6], 71), 0)
    down_weight = scatter_about(key_of[3], (F, D), F ** -0.5, 0.0625, ((0, 4),))
    noise_up = scatter_about(key_of[4], (D, F), 1.0, 6.0, ((0, 8), (1, 4)), jnp.float32)
    noise_down = scatter_about(key_of[5], (F, D), 1.0, 6.0, ((0, 4), (1, 8)), jnp.float32)
    return {"hidden_in": hidden_in, "target": target, "up_weight": up_weight, "down_weight": down_weight, "noise_up": noise_up, "noise_down": noise_down}


local_rate = 0.5
clip_rms = 0.08
server_rate = 0.02

def gelu_back(pre, back):
    return jax.vjp(lambda value: jax.nn.gelu(value, approximate=True), pre)[1](back)[0]

def gradients(inputs, goals, w_up, w_down):
    xfloat = inputs.astype(jnp.float32)
    normed = (xfloat * lax.rsqrt(lax.optimization_barrier(jnp.mean(xfloat * xfloat, axis=-1, keepdims=True)) + 1e-06)).astype(jnp.bfloat16)
    pre = jnp.dot(normed, w_up, preferred_element_type=jnp.float32)
    act = jax.nn.gelu(pre, approximate=True).astype(jnp.bfloat16)
    output = xfloat + jnp.dot(act, w_down, preferred_element_type=jnp.float32)
    resid = ((output - goals.astype(jnp.float32)) / inputs.shape[0]).astype(jnp.bfloat16)
    grad_down = jnp.dot(act.T, resid, preferred_element_type=jnp.float32)
    back = jnp.dot(resid, w_down.T, preferred_element_type=jnp.float32)
    dpre = gelu_back(pre, back).astype(jnp.bfloat16)
    grad_up = jnp.dot(normed.T, dpre, preferred_element_type=jnp.float32)
    return (grad_up, grad_down)

def reference(hidden_in, target, up_weight, down_weight, noise_up, noise_down):
    bound = clip_rms * math.sqrt(2.0 * D * F)

    def per_client(carry, pair):
        inputs, goals = pair
        w_up, w_down = (up_weight, down_weight)
        acc_up = jnp.zeros((D, F), jnp.float32)
        acc_down = jnp.zeros((F, D), jnp.float32)
        for turn in range(STEPS):
            grad_up, grad_down = gradients(inputs[turn], goals[turn], w_up, w_down)
            acc_up = acc_up + grad_up
            acc_down = acc_down + grad_down
            w_up = (w_up.astype(jnp.float32) - local_rate * grad_up).astype(jnp.bfloat16)
            w_down = (w_down.astype(jnp.float32) - local_rate * grad_down).astype(jnp.bfloat16)
        delta_up = -local_rate * acc_up
        delta_down = -local_rate * acc_down
        size = jnp.sqrt(jnp.sum(delta_up * delta_up) + jnp.sum(delta_down * delta_down))
        factor = bound / jnp.maximum(size, bound)
        clip_up = lax.optimization_barrier((delta_up * factor).astype(jnp.bfloat16)).astype(jnp.float32)
        clip_down = lax.optimization_barrier((delta_down * factor).astype(jnp.bfloat16)).astype(jnp.float32)
        return ((carry[0] + clip_up, carry[1] + clip_down), None)
    start = (jnp.zeros((D, F), jnp.float32), jnp.zeros((F, D), jnp.float32))
    totals, unused = lax.scan(per_client, start, (hidden_in, target))
    root = math.sqrt(N_CLIENT * N_REGION)
    scale = server_rate / (clip_rms * root)
    new_up = up_weight.astype(jnp.float32) + scale * (totals[0] + clip_rms * root * noise_up)
    new_down = down_weight.astype(jnp.float32) + scale * (totals[1] + clip_rms * root * noise_down)
    return (new_up, new_down)
```

```python
import math

import jax
import jax.numpy as jnp
from jax import lax
from jax.sharding import PartitionSpec as P

D = 1792
F = 7168
STEPS = 2


local_rate = 0.5
clip_rms = 0.08
server_rate = 0.02


def gelu_back(pre, back):
    return jax.vjp(lambda value: jax.nn.gelu(value, approximate=True), pre)[1](back)[0]


def contract_rows(left, right):
    return lax.dot_general(
        left, right, (((0,), (0,)), ((), ())), preferred_element_type=jnp.float32
    )


def shards(hidden_in, target, up_weight, down_weight, noise_up, noise_down):
    inputs_all, goals_all = (
        lax.all_gather(hidden_in, "tp", axis=3, tiled=True),
        lax.all_gather(target, "tp", axis=3, tiled=True),
    )
    inputs_all = inputs_all[0]
    goals_all = goals_all[0]
    w_up, w_down = (up_weight, down_weight)
    acc_up = jnp.zeros(up_weight.shape, jnp.float32)
    acc_down = jnp.zeros(down_weight.shape, jnp.float32)
    for turn in range(STEPS):
        inputs = inputs_all[turn]
        xfloat = inputs.astype(jnp.float32)
        normed = (
            xfloat * lax.rsqrt(jnp.mean(xfloat * xfloat, axis=-1, keepdims=True) + 1e-06)
        ).astype(jnp.bfloat16)
        pre = jnp.dot(normed, w_up, preferred_element_type=jnp.float32)
        act = jax.nn.gelu(pre, approximate=True).astype(jnp.bfloat16)
        partial_out = jnp.dot(act, w_down, preferred_element_type=jnp.float32)
        output = xfloat + lax.psum(partial_out.astype(jnp.bfloat16), "tp").astype(jnp.float32)
        resid = ((output - goals_all[turn].astype(jnp.float32)) / inputs.shape[0]).astype(
            jnp.bfloat16
        )
        grad_down = contract_rows(act, resid)
        back = lax.dot_general(
            resid, w_down, (((1,), (1,)), ((), ())), preferred_element_type=jnp.float32
        )
        dpre = gelu_back(pre, back).astype(jnp.bfloat16)
        grad_up = contract_rows(normed, dpre)
        acc_up = acc_up + grad_up
        acc_down = acc_down + grad_down
        if turn + 1 < STEPS:
            w_up = (w_up.astype(jnp.float32) - local_rate * grad_up).astype(jnp.bfloat16)
            w_down = (w_down.astype(jnp.float32) - local_rate * grad_down).astype(jnp.bfloat16)
    delta_up = -local_rate * acc_up
    delta_down = -local_rate * acc_down
    squared = lax.psum(jnp.sum(delta_up * delta_up) + jnp.sum(delta_down * delta_down), "tp")
    bound = clip_rms * math.sqrt(2.0 * D * F)
    factor = bound / jnp.maximum(jnp.sqrt(squared), bound)
    clip_up = lax.optimization_barrier((delta_up * factor).astype(jnp.bfloat16)).astype(jnp.float32)
    clip_down = lax.optimization_barrier((delta_down * factor).astype(jnp.bfloat16)).astype(
        jnp.float32
    )
    summed_up, summed_down = (
        lax.psum_scatter(
            clip_up.astype(jnp.bfloat16), "client", scatter_dimension=0, tiled=True
        ).astype(jnp.float32),
        lax.psum_scatter(
            clip_down.astype(jnp.bfloat16), "client", scatter_dimension=1, tiled=True
        ).astype(jnp.float32),
    )
    client_count = lax.axis_size("client")
    region_count = lax.axis_size("region")
    count = client_count * region_count
    rows = D // count
    region_index = lax.axis_index("region")
    full_up, full_down = (
        lax.psum(summed_up.astype(jnp.bfloat16), "region").astype(jnp.float32),
        lax.psum(summed_down.astype(jnp.bfloat16), "region").astype(jnp.float32),
    )
    share_up = lax.dynamic_slice_in_dim(full_up, region_index * rows, rows, 0)
    share_down = lax.dynamic_slice_in_dim(full_down, region_index * rows, rows, 1)
    block = lax.axis_index("client") * region_count + region_index
    base_up = lax.dynamic_slice_in_dim(up_weight, block * rows, rows, 0).astype(jnp.float32)
    base_down = lax.dynamic_slice_in_dim(down_weight, block * rows, rows, 1).astype(jnp.float32)
    root = math.sqrt(count)
    scale = server_rate / (clip_rms * root)
    new_up = base_up + scale * (share_up + clip_rms * root * noise_up)
    new_down = base_down + scale * (share_down + clip_rms * root * noise_down)
    return (new_up, new_down)


def dot(left, right):
    return jnp.dot(left, right, preferred_element_type=jnp.float32)


def dot_t(left, right):
    return lax.dot_general(
        left,
        right,
        (((left.ndim - 1,), (right.ndim - 1,)), (tuple(range(left.ndim - 2)),) * 2),
        preferred_element_type=jnp.float32,
    )


def gelu(pre):
    return jax.nn.gelu(pre, approximate=True).astype(jnp.bfloat16)


def normalise(inputs):
    xfloat = inputs.astype(jnp.float32)
    return (
        xfloat * lax.rsqrt(jnp.mean(xfloat * xfloat, axis=-1, keepdims=True) + 1e-06)
    ).astype(jnp.bfloat16)


def recomputed(hidden_in, target, up_weight, down_weight, noise_up, noise_down):
    both = lax.all_gather(
        jnp.concatenate([hidden_in, target], 0), "tp", axis=3, tiled=True
    )
    inputs, goals = both[0], both[1]
    tokens = inputs.shape[1]
    clients = ("client", "region")
    every = lax.all_gather(inputs, clients)
    normed = normalise(inputs)

    def residual(partial_out, turn):
        output = inputs[turn].astype(jnp.float32) + lax.psum(
            partial_out.astype(jnp.bfloat16), "tp"
        ).astype(jnp.float32)
        return ((output - goals[turn].astype(jnp.float32)) / tokens).astype(jnp.bfloat16)

    pre0 = dot(normed[0], up_weight)
    act0 = gelu(pre0)
    resid0 = residual(dot(act0, down_weight), 0)
    every_resid0 = lax.all_gather(resid0, clients)
    dpre0 = gelu_back(pre0, dot_t(resid0, down_weight)).astype(jnp.bfloat16)
    overlap = (local_rate * dot_t(normed[1], normed[0])).astype(jnp.bfloat16)
    act1 = gelu(dot(normed[1], up_weight) - dot(overlap, dpre0))
    overlap = (local_rate * dot_t(act1, act0)).astype(jnp.bfloat16)
    resid1 = residual(dot(act1, down_weight) - dot(overlap, resid0), 1)
    every_resid1 = lax.all_gather(resid1, clients)

    count = every.shape[0]
    every_normed = normalise(every)
    first, second = every_normed[:, 0], every_normed[:, 1]
    pre0 = dot(first, up_weight)
    act0 = gelu(pre0)
    dpre0 = gelu_back(pre0, dot_t_flat(every_resid0, down_weight)).astype(jnp.bfloat16)
    overlap = (local_rate * dot_t(second, first)).astype(jnp.bfloat16)
    pre1 = dot(second, up_weight) - batched(overlap, dpre0)
    act1 = gelu(pre1)
    overlap = (local_rate * dot_t(every_resid1, every_resid0)).astype(jnp.bfloat16)
    back1 = dot_t_flat(every_resid1, down_weight) - batched(overlap, act0)
    dpre1 = gelu_back(pre1, back1).astype(jnp.bfloat16)

    rows_n = every_normed.reshape(count, STEPS * tokens, -1)
    rows_r = jnp.concatenate([every_resid0, every_resid1], 1)
    rows_a = jnp.concatenate([act0, act1], 1)
    rows_p = jnp.concatenate([dpre0, dpre1], 1)
    squared = jnp.sum(
        dot_t(rows_n, rows_n) * dot_t(rows_p, rows_p)
        + dot_t(rows_a, rows_a) * dot_t(rows_r, rows_r),
        axis=(1, 2),
    )
    size = local_rate * jnp.sqrt(jnp.maximum(lax.psum(squared, "tp"), 0.0))
    bound = clip_rms * math.sqrt(2.0 * D * F)
    factor = (-local_rate * bound / jnp.maximum(size, bound))[:, None, None]

    share = D // count
    block = lax.axis_index("client") * lax.axis_size("region") + lax.axis_index("region")

    def own(rows):
        part = lax.dynamic_slice_in_dim(rows, block * share, share, 2)
        return (part.astype(jnp.float32) * factor).astype(jnp.bfloat16).reshape(-1, share)

    total_up = contract_rows(own(rows_n), rows_p.reshape(count * STEPS * tokens, -1))
    total_down = contract_rows(rows_a.reshape(count * STEPS * tokens, -1), own(rows_r))
    base_up = lax.dynamic_slice_in_dim(up_weight, block * share, share, 0).astype(jnp.float32)
    base_down = lax.dynamic_slice_in_dim(down_weight, block * share, share, 1).astype(jnp.float32)
    root = math.sqrt(count)
    scale = server_rate / (clip_rms * root)
    return (
        base_up + scale * (total_up + clip_rms * root * noise_up),
        base_down + scale * (total_down + clip_rms * root * noise_down),
    )


def dot_t_flat(left, right):
    return lax.dot_general(
        left, right, (((left.ndim - 1,), (1,)), ((), ())), preferred_element_type=jnp.float32
    )


def batched(left, right):
    return lax.dot_general(
        left, right, (((2,), (1,)), ((0,), (0,))), preferred_element_type=jnp.float32
    )


def solution(mesh):
    few = mesh.shape["client"] * mesh.shape["region"] <= 8
    body = recomputed if few else shards
    placed = (
        P(("client", "region"), None, None, "tp"),
        P(("client", "region"), None, None, "tp"),
        P(None, "tp"),
        P("tp", None),
        P(("client", "region"), "tp"),
        P("tp", ("client", "region")),
    )
    return jax.shard_map(
        body,
        mesh=mesh,
        in_specs=placed,
        out_specs=(P(("client", "region"), "tp"), P("tp", ("client", "region"))),
        check_vma=False,
    )
```

```python
import functools
import math

import jax
import jax.numpy as jnp
from jax import lax
from jax.experimental import pallas as pl
from jax.experimental.pallas import tpu as pltpu
from jax.sharding import PartitionSpec as P

D = 1792
F = 7168
STEPS = 2


local_rate = 0.5
clip_rms = 0.08
server_rate = 0.02


def gelu_back(pre, back):
    return jax.vjp(lambda value: jax.nn.gelu(value, approximate=True), pre)[1](back)[0]


def contract_rows(left, right):
    return lax.dot_general(
        left, right, (((0,), (0,)), ((), ())), preferred_element_type=jnp.float32
    )


def shards(hidden_in, target, up_weight, down_weight, noise_up, noise_down):
    inputs_all, goals_all = (
        lax.all_gather(hidden_in, "tp", axis=3, tiled=True),
        lax.all_gather(target, "tp", axis=3, tiled=True),
    )
    inputs_all = inputs_all[0]
    goals_all = goals_all[0]
    w_up, w_down = (up_weight, down_weight)
    acc_up = jnp.zeros(up_weight.shape, jnp.float32)
    acc_down = jnp.zeros(down_weight.shape, jnp.float32)
    for turn in range(STEPS):
        inputs = inputs_all[turn]
        xfloat = inputs.astype(jnp.float32)
        normed = (
            xfloat * lax.rsqrt(jnp.mean(xfloat * xfloat, axis=-1, keepdims=True) + 1e-06)
        ).astype(jnp.bfloat16)
        pre = jnp.dot(normed, w_up, preferred_element_type=jnp.float32)
        act = jax.nn.gelu(pre, approximate=True).astype(jnp.bfloat16)
        partial_out = jnp.dot(act, w_down, preferred_element_type=jnp.float32)
        output = xfloat + lax.psum(partial_out.astype(jnp.bfloat16), "tp").astype(jnp.float32)
        resid = ((output - goals_all[turn].astype(jnp.float32)) / inputs.shape[0]).astype(
            jnp.bfloat16
        )
        grad_down = contract_rows(act, resid)
        back = lax.dot_general(
            resid, w_down, (((1,), (1,)), ((), ())), preferred_element_type=jnp.float32
        )
        dpre = gelu_back(pre, back).astype(jnp.bfloat16)
        grad_up = contract_rows(normed, dpre)
        acc_up = acc_up + grad_up
        acc_down = acc_down + grad_down
        if turn + 1 < STEPS:
            w_up = (w_up.astype(jnp.float32) - local_rate * grad_up).astype(jnp.bfloat16)
            w_down = (w_down.astype(jnp.float32) - local_rate * grad_down).astype(jnp.bfloat16)
    delta_up = -local_rate * acc_up
    delta_down = -local_rate * acc_down
    squared = lax.psum(jnp.sum(delta_up * delta_up) + jnp.sum(delta_down * delta_down), "tp")
    bound = clip_rms * math.sqrt(2.0 * D * F)
    factor = bound / jnp.maximum(jnp.sqrt(squared), bound)
    clip_up = lax.optimization_barrier((delta_up * factor).astype(jnp.bfloat16)).astype(jnp.float32)
    clip_down = lax.optimization_barrier((delta_down * factor).astype(jnp.bfloat16)).astype(
        jnp.float32
    )
    summed_up, summed_down = (
        lax.psum_scatter(
            clip_up.astype(jnp.bfloat16), "client", scatter_dimension=0, tiled=True
        ).astype(jnp.float32),
        lax.psum_scatter(
            clip_down.astype(jnp.bfloat16), "client", scatter_dimension=1, tiled=True
        ).astype(jnp.float32),
    )
    client_count = lax.axis_size("client")
    region_count = lax.axis_size("region")
    count = client_count * region_count
    rows = D // count
    region_index = lax.axis_index("region")
    full_up, full_down = (
        lax.psum(summed_up.astype(jnp.bfloat16), "region").astype(jnp.float32),
        lax.psum(summed_down.astype(jnp.bfloat16), "region").astype(jnp.float32),
    )
    share_up = lax.dynamic_slice_in_dim(full_up, region_index * rows, rows, 0)
    share_down = lax.dynamic_slice_in_dim(full_down, region_index * rows, rows, 1)
    block = lax.axis_index("client") * region_count + region_index
    base_up = lax.dynamic_slice_in_dim(up_weight, block * rows, rows, 0).astype(jnp.float32)
    base_down = lax.dynamic_slice_in_dim(down_weight, block * rows, rows, 1).astype(jnp.float32)
    root = math.sqrt(count)
    scale = server_rate / (clip_rms * root)
    new_up = base_up + scale * (share_up + clip_rms * root * noise_up)
    new_down = base_down + scale * (share_down + clip_rms * root * noise_down)
    return (new_up, new_down)


MESH = pl.DeviceIdType.MESH
WIDE = 256


def dot(left, right):
    return jnp.dot(left, right, preferred_element_type=jnp.float32)


def dot_t(left, right):
    return lax.dot_general(
        left, right, (((1,), (1,)), ((), ())), preferred_element_type=jnp.float32
    )


def gelu_pair(pre):
    root = math.sqrt(2.0 / math.pi)
    square = pre * pre
    bent = jnp.tanh(root * (pre + 0.044715 * (square * pre)))
    half = 0.5 * (1.0 + bent)
    slope = half + 0.5 * pre * (1.0 - bent * bent) * (root * (1.0 + 0.134145 * square))
    return pre * half, slope


def round_kernel(
    sizes,
    hidden,
    goal,
    up_hbm,
    down_hbm,
    out_up,
    out_down,
    up,
    down,
    shares,
    goals,
    own_x,
    normed,
    resid0,
    resid1,
    acts,
    dpres,
    picked_n,
    picked_r,
    later_pre,
    total,
    sent,
    landed,
    squares,
    local_sems,
    in_s,
    in_r,
    sum_s,
    sum_r,
    z_s,
    z_r,
    y_s,
    y_r,
    core_s,
    core_r,
    tp_s,
    tp_r,
):
    n_tp, n_c, n_r = sizes
    bf16, f32 = jnp.bfloat16, jnp.float32
    tp, c, r = lax.axis_index("tp"), lax.axis_index("client"), lax.axis_index("region")
    tokens, width = own_x.shape[0] // STEPS, own_x.shape[1]
    local = up.shape[1]
    blocks = local // WIDE
    rows = tokens // n_tp
    part = width // 2
    core = lax.rem(tp, 2)
    core_peer = {"tp": tp + 1 - 2 * core}
    y_peer = {"region": 1 - r}
    me = c * n_r + r
    count = n_c * n_r

    def remote(src, dst, send, recv, peer):
        return pltpu.make_async_remote_copy(
            src_ref=src, dst_ref=dst, send_sem=send, recv_sem=recv, device_id=peer,
            device_id_type=MESH,
        )

    def tp_peer(d):
        return lax.rem(tp + d, n_tp)

    def tp_from(d):
        return lax.rem(tp + n_tp - d, n_tp)

    def c_from(d):
        return lax.rem(c + n_c - d, n_c)

    load_up = pltpu.make_async_copy(up_hbm, up, local_sems.at[0])
    load_down = pltpu.make_async_copy(down_hbm, down, local_sems.at[1])
    load_up.start()
    load_down.start()

    barrier = pltpu.get_barrier_semaphore()
    for d in range(1, n_tp):
        pl.semaphore_signal(barrier, inc=1, device_id={"tp": tp_peer(d)}, device_id_type=MESH)
    for d in range(1, n_c):
        pl.semaphore_signal(
            barrier, inc=1, device_id={"client": lax.rem(c + d, n_c)}, device_id_type=MESH
        )
    pl.semaphore_signal(barrier, inc=1, device_id=y_peer, device_id_type=MESH)
    pl.semaphore_wait(barrier, n_tp + n_c - 1)

    pending = []

    def start(copy):
        copy.start()
        pending.append(copy)
        return copy

    for d in range(1, n_tp):
        start(remote(hidden, shares.at[tp], in_s.at[0, d], in_r.at[0, d], {"tp": tp_peer(d)}))
    for d in range(1, n_tp):
        to = pl.multiple_of(tp_peer(d) * rows, rows)
        start(
            remote(
                goal.at[:, pl.ds(to, rows), :], goals.at[tp], in_s.at[1, d], in_r.at[1, d],
                {"tp": tp_peer(d)},
            )
        )
    shares[tp] = hidden[...]
    mine = pl.multiple_of(tp * rows, rows)
    goals[tp] = goal[:, pl.ds(mine, rows), :]
    for d in range(1, n_tp):
        slot = shares.at[tp_from(d)]
        remote(slot, slot, in_s.at[0, d], in_r.at[0, d], {"tp": tp_from(d)}).wait_recv()
    xfloat = jnp.concatenate([shares[j].astype(f32) for j in range(n_tp)], axis=-1)
    xfloat = xfloat.reshape(STEPS * tokens, width)
    own_x[...] = xfloat.astype(bf16)
    normed[me] = (
        xfloat * lax.rsqrt(jnp.mean(xfloat * xfloat, axis=-1, keepdims=True) + 1e-06)
    ).astype(bf16)

    def half(ref, k, which):
        return ref.at[k, :, pl.ds(pl.multiple_of(which * part, part), part)]

    def z_start(ref, p):
        for d in range(1, n_c):
            block = half(ref, me, core)
            start(
                remote(
                    block, block, z_s.at[p, d], z_r.at[p, d], {"client": lax.rem(c + d, n_c)}
                )
            )
        block = half(ref, me, core)
        start(remote(block, block, y_s.at[p, 0], y_r.at[p, 0], y_peer))

    def z_end(ref, p):
        for d in range(1, n_c):
            k = c_from(d) * n_r + r
            block = half(ref, k, core)
            remote(
                block, block, z_s.at[p, d], z_r.at[p, d], {"client": c_from(d)}
            ).wait_recv()
            start(remote(block, block, y_s.at[p, d], y_r.at[p, d], y_peer))
            start(remote(block, block, core_s.at[p, d], core_r.at[p, d], core_peer))

    def y_end(ref, p):
        for d in range(n_c):
            k = c_from(d) * n_r + (1 - r)
            block = half(ref, k, core)
            remote(block, block, y_s.at[p, d], y_r.at[p, d], y_peer).wait_recv()
            start(remote(block, block, core_s.at[p, n_c + d], core_r.at[p, n_c + d], core_peer))

    def core_end(ref, p):
        for d in range(1, 2 * n_c):
            k = c_from(d % n_c) * n_r + (r if d < n_c else 1 - r)
            block = half(ref, k, 1 - core)
            remote(block, block, core_s.at[p, d], core_r.at[p, d], core_peer).wait_recv()

    z_start(normed, 0)

    def columns(b):
        return pl.ds(pl.multiple_of(b * WIDE, WIDE), WIDE)

    total[...] = jnp.zeros_like(total)
    load_up.wait()
    load_down.wait()

    def first(b, unused):
        at = columns(b)
        pre = dot(normed[me], up[:, at])
        later_pre[:, at] = pre[tokens:]
        act, slope = gelu_pair(pre[:tokens])
        act = act.astype(bf16)
        acts[me, :tokens, at] = act
        dpres[me, :tokens, at] = slope.astype(bf16)
        total[...] += dot(act, down[at, :])
        return unused

    lax.fori_loop(0, blocks, first, 0)
    overlap_n = (local_rate * dot_t(normed[me, tokens:], normed[me, :tokens])).astype(bf16)

    for d in range(1, n_tp):
        slot = goals.at[tp_from(d)]
        remote(slot, slot, in_s.at[1, d], in_r.at[1, d], {"tp": tp_from(d)}).wait_recv()
    goal_rows = jnp.concatenate([goals[j].astype(f32) for j in range(n_tp)], axis=-1)

    def residual(step, ref):
        sent[step] = total[...].astype(bf16)
        for d in range(1, n_tp):
            to = pl.multiple_of(tp_peer(d) * rows, rows)
            start(
                remote(
                    sent.at[step, pl.ds(to, rows), :], landed.at[step, d - 1],
                    sum_s.at[2 * step, d], sum_r.at[2 * step, d], {"tp": tp_peer(d)},
                )
            )
        output = total[pl.ds(mine, rows), :]
        for d in range(1, n_tp):
            slot = landed.at[step, d - 1]
            remote(
                slot, slot, sum_s.at[2 * step, d], sum_r.at[2 * step, d], {"tp": tp_from(d)}
            ).wait_recv()
            output = output + landed[step, d - 1].astype(f32)
        held = own_x[pl.ds(pl.multiple_of(step * tokens + tp * rows, rows), rows), :]
        output = output + held.astype(f32)
        ref[me, pl.ds(mine, rows), :] = ((output - goal_rows[step]) / tokens).astype(bf16)
        for d in range(1, n_tp):
            slot = ref.at[me, pl.ds(mine, rows), :]
            start(
                remote(
                    slot, slot, sum_s.at[2 * step + 1, d], sum_r.at[2 * step + 1, d],
                    {"tp": tp_peer(d)},
                )
            )
        for d in range(1, n_tp):
            slot = ref.at[me, pl.ds(pl.multiple_of(tp_from(d) * rows, rows), rows), :]
            remote(
                slot, slot, sum_s.at[2 * step + 1, d], sum_r.at[2 * step + 1, d],
                {"tp": tp_from(d)},
            ).wait_recv()

    residual(0, resid0)
    z_start(resid0, 1)
    z_end(normed, 0)

    total[...] = jnp.zeros_like(total)

    def second(b, overlap_a):
        at = columns(b)
        back = dot_t(resid0[me], down[at, :])
        dpre = (back * dpres[me, :tokens, at].astype(f32)).astype(bf16)
        dpres[me, :tokens, at] = dpre
        act, slope = gelu_pair(later_pre[:, at] - dot(overlap_n, dpre))
        act = act.astype(bf16)
        acts[me, tokens:, at] = act
        dpres[me, tokens:, at] = slope.astype(bf16)
        total[...] += dot(act, down[at, :])
        return overlap_a + dot_t(act, acts[me, :tokens, at])

    overlap_a = lax.fori_loop(0, blocks, second, jnp.zeros((tokens, tokens), f32))
    total[...] -= dot((local_rate * overlap_a).astype(bf16), resid0[me])
    y_end(normed, 0)
    residual(1, resid1)
    z_start(resid1, 2)
    z_end(resid0, 1)

    chosen = (
        lax.broadcasted_iota(jnp.int32, (WIDE, width), 1)
        == lax.broadcasted_iota(jnp.int32, (WIDE, width), 0) + me * (width // count)
    )
    chosen = jnp.where(chosen, 1.0, 0.0).astype(bf16)

    def last_back(k):
        overlap_r = (local_rate * dot_t(resid1[k], resid0[k])).astype(bf16)

        def body(b, unused):
            at = columns(b)
            back = dot_t(resid1[k], down[at, :]) - dot(overlap_r, acts[k, :tokens, at])
            dpres[k, tokens:, at] = (back * dpres[k, tokens:, at].astype(f32)).astype(bf16)
            return unused

        lax.fori_loop(0, blocks, body, 0)
        picked_r[k, :, :tokens] = dot_t(chosen, resid0[k]).astype(bf16)
        picked_r[k, :, tokens:] = dot_t(chosen, resid1[k]).astype(bf16)

    last_back(me)
    picked_n[me] = dot_t(chosen, normed[me]).astype(bf16)
    rows_r = jnp.concatenate([resid0[me], resid1[me]], axis=0)
    products = dot_t(normed[me], normed[me]) * dot_t(dpres[me], dpres[me])
    products = products + dot_t(acts[me], acts[me]) * dot_t(rows_r, rows_r)
    squares[tp, me] = jnp.broadcast_to(jnp.sum(products, keepdims=True), squares.shape[2:])
    for d in range(1, n_c):
        slot = squares.at[tp, me]
        start(
            remote(slot, slot, z_s.at[3, d], z_r.at[3, d], {"client": lax.rem(c + d, n_c)})
        )
    slot = squares.at[tp, me]
    start(remote(slot, slot, y_s.at[3, 0], y_r.at[3, 0], y_peer))

    y_end(resid0, 1)
    z_end(resid1, 2)
    core_end(normed, 0)
    core_end(resid0, 1)

    def early(j, unused):
        k = lax.rem(me + j, count)
        overlap = (local_rate * dot_t(normed[k, tokens:], normed[k, :tokens])).astype(bf16)

        def body(b, unused):
            at = columns(b)
            pre = dot(normed[k], up[:, at])
            back = dot_t(resid0[k], down[at, :])
            act, slope = gelu_pair(pre[:tokens])
            acts[k, :tokens, at] = act.astype(bf16)
            dpre = (back * slope).astype(bf16)
            dpres[k, :tokens, at] = dpre
            act, slope = gelu_pair(pre[tokens:] - dot(overlap, dpre))
            acts[k, tokens:, at] = act.astype(bf16)
            dpres[k, tokens:, at] = slope.astype(bf16)
            return unused

        lax.fori_loop(0, blocks, body, 0)
        picked_n[k] = dot_t(chosen, normed[k]).astype(bf16)
        return unused

    lax.fori_loop(1, count // 2, early, 0)
    y_end(resid1, 2)
    for d in range(1, n_c):
        slot = squares.at[tp, c_from(d) * n_r + r]
        remote(slot, slot, z_s.at[3, d], z_r.at[3, d], {"client": c_from(d)}).wait_recv()
        start(remote(slot, slot, y_s.at[3, d], y_r.at[3, d], y_peer))
    lax.fori_loop(count // 2, count, early, 0)
    for d in range(n_c):
        slot = squares.at[tp, c_from(d) * n_r + (1 - r)]
        remote(slot, slot, y_s.at[3, d], y_r.at[3, d], y_peer).wait_recv()
    for d in range(1, n_tp):
        slot = squares.at[tp]
        start(remote(slot, slot, tp_s.at[d], tp_r.at[d], {"tp": tp_peer(d)}))
    core_end(resid1, 2)

    def late(j, unused):
        last_back(lax.rem(me + j, count))
        return unused

    lax.fori_loop(1, count, late, 0)
    for d in range(1, n_tp):
        slot = squares.at[tp_from(d)]
        remote(slot, slot, tp_s.at[d], tp_r.at[d], {"tp": tp_from(d)}).wait_recv()

    out_up[...] = jnp.zeros_like(out_up)
    out_down[...] = jnp.zeros_like(out_down)
    bound = clip_rms * math.sqrt(2.0 * width * local * n_tp)

    def add(k, unused):
        square = squares[0, k]
        for t in range(1, n_tp):
            square = square + squares[t, k]
        size = local_rate * jnp.sqrt(jnp.maximum(square, 0.0))
        factor = (-local_rate * bound / jnp.maximum(size, bound))[:1]
        left = (picked_n[k].astype(f32) * factor).astype(bf16)
        out_up[...] += dot(left, dpres[k])
        left = (picked_r[k].astype(f32) * factor).astype(bf16)
        out_down[...] += dot(left, acts[k])
        return unused

    lax.fori_loop(0, count, add, 0)
    for copy in pending:
        copy.wait_send()


def gathered(sizes, hidden_in, target, up_weight, down_weight, noise_up, noise_down):
    n_tp, n_c, n_r = sizes
    count = n_c * n_r
    steps, tokens, share = hidden_in.shape[1:]
    width, local = up_weight.shape
    both = steps * tokens
    bf16, f32 = jnp.bfloat16, jnp.float32
    vmem = pl.BlockSpec(memory_space=pltpu.VMEM)
    dma = pltpu.SemaphoreType.DMA
    total_up, total_down = pl.pallas_call(
        functools.partial(round_kernel, sizes),
        out_shape=[jax.ShapeDtypeStruct((WIDE, local), f32)] * 2,
        in_specs=[vmem, vmem] + [pl.BlockSpec(memory_space=pl.ANY)] * 2,
        out_specs=[vmem, vmem],
        scratch_shapes=[
            pltpu.VMEM((width, local), bf16),
            pltpu.VMEM((local, width), bf16),
            pltpu.VMEM((n_tp, steps, tokens, share), bf16),
            pltpu.VMEM((n_tp, steps, tokens // n_tp, share), bf16),
            pltpu.VMEM((both, width), bf16),
            pltpu.VMEM((count, both, width), bf16),
            pltpu.VMEM((count, tokens, width), bf16),
            pltpu.VMEM((count, tokens, width), bf16),
            pltpu.VMEM((count, both, local), bf16),
            pltpu.VMEM((count, both, local), bf16),
            pltpu.VMEM((count, WIDE, both), bf16),
            pltpu.VMEM((count, WIDE, both), bf16),
            pltpu.VMEM((tokens, local), f32),
            pltpu.VMEM((tokens, width), f32),
            pltpu.VMEM((steps, tokens, width), bf16),
            pltpu.VMEM((steps, n_tp - 1, tokens // n_tp, width), bf16),
            pltpu.VMEM((n_tp, count, 8, both), f32),
            dma((2,)),
            dma((2, n_tp)),
            dma((2, n_tp)),
            dma((2 * steps, n_tp)),
            dma((2 * steps, n_tp)),
            dma((4, n_c)),
            dma((4, n_c)),
            dma((4, n_c)),
            dma((4, n_c)),
            dma((3, 2 * n_c)),
            dma((3, 2 * n_c)),
            dma((n_tp,)),
            dma((n_tp,)),
        ],
        compiler_params=pltpu.CompilerParams(
            collective_id=0, has_side_effects=True, vmem_limit_bytes=62 * 1024 * 1024
        ),
    )(hidden_in[0], target[0], up_weight, down_weight)

    rows = width // count
    block = lax.axis_index("client") * n_r + lax.axis_index("region")
    base_up = lax.dynamic_slice_in_dim(up_weight, block * rows, rows, 0).astype(f32)
    base_down = lax.dynamic_slice_in_dim(down_weight, block * rows, rows, 1).astype(f32)
    root = math.sqrt(count)
    scale = server_rate / (clip_rms * root)
    return (
        base_up + scale * (total_up[:rows] + clip_rms * root * noise_up),
        base_down + scale * (total_down[:rows].T + clip_rms * root * noise_down),
    )


def solution(mesh):
    sizes = tuple(mesh.shape[axis] for axis in ("tp", "client", "region"))
    few = sizes[1] * sizes[2] <= 8 and sizes[2] == 2 and sizes[0] % 2 == 0
    body = functools.partial(gathered, sizes) if few else shards
    placed = (
        P(("client", "region"), None, None, "tp"),
        P(("client", "region"), None, None, "tp"),
        P(None, "tp"),
        P("tp", None),
        P(("client", "region"), "tp"),
        P("tp", ("client", "region")),
    )
    return jax.shard_map(
        body,
        mesh=mesh,
        in_specs=placed,
        out_specs=(P(("client", "region"), "tp"), P("tp", ("client", "region"))),
        check_vma=False,
    )
```

```python
import functools
import math

import jax
import jax.numpy as jnp
from jax import lax
from jax.experimental import pallas as pl
from jax.experimental.pallas import tpu as pltpu
from jax.sharding import PartitionSpec as P

D = 1792
F = 7168
STEPS = 2


local_rate = 0.5
clip_rms = 0.08
server_rate = 0.02


def gelu_back(pre, back):
    return jax.vjp(lambda value: jax.nn.gelu(value, approximate=True), pre)[1](back)[0]


def contract_rows(left, right):
    return lax.dot_general(
        left, right, (((0,), (0,)), ((), ())), preferred_element_type=jnp.float32
    )


def shards(hidden_in, target, up_weight, down_weight, noise_up, noise_down):
    inputs_all, goals_all = (
        lax.all_gather(hidden_in, "tp", axis=3, tiled=True),
        lax.all_gather(target, "tp", axis=3, tiled=True),
    )
    inputs_all = inputs_all[0]
    goals_all = goals_all[0]
    w_up, w_down = (up_weight, down_weight)
    acc_up = jnp.zeros(up_weight.shape, jnp.float32)
    acc_down = jnp.zeros(down_weight.shape, jnp.float32)
    for turn in range(STEPS):
        inputs = inputs_all[turn]
        xfloat = inputs.astype(jnp.float32)
        normed = (
            xfloat * lax.rsqrt(jnp.mean(xfloat * xfloat, axis=-1, keepdims=True) + 1e-06)
        ).astype(jnp.bfloat16)
        pre = jnp.dot(normed, w_up, preferred_element_type=jnp.float32)
        act = jax.nn.gelu(pre, approximate=True).astype(jnp.bfloat16)
        partial_out = jnp.dot(act, w_down, preferred_element_type=jnp.float32)
        output = xfloat + lax.psum(partial_out.astype(jnp.bfloat16), "tp").astype(jnp.float32)
        resid = ((output - goals_all[turn].astype(jnp.float32)) / inputs.shape[0]).astype(
            jnp.bfloat16
        )
        grad_down = contract_rows(act, resid)
        back = lax.dot_general(
            resid, w_down, (((1,), (1,)), ((), ())), preferred_element_type=jnp.float32
        )
        dpre = gelu_back(pre, back).astype(jnp.bfloat16)
        grad_up = contract_rows(normed, dpre)
        acc_up = acc_up + grad_up
        acc_down = acc_down + grad_down
        if turn + 1 < STEPS:
            w_up = (w_up.astype(jnp.float32) - local_rate * grad_up).astype(jnp.bfloat16)
            w_down = (w_down.astype(jnp.float32) - local_rate * grad_down).astype(jnp.bfloat16)
    delta_up = -local_rate * acc_up
    delta_down = -local_rate * acc_down
    squared = lax.psum(jnp.sum(delta_up * delta_up) + jnp.sum(delta_down * delta_down), "tp")
    bound = clip_rms * math.sqrt(2.0 * D * F)
    factor = bound / jnp.maximum(jnp.sqrt(squared), bound)
    clip_up = lax.optimization_barrier((delta_up * factor).astype(jnp.bfloat16)).astype(jnp.float32)
    clip_down = lax.optimization_barrier((delta_down * factor).astype(jnp.bfloat16)).astype(
        jnp.float32
    )
    summed_up, summed_down = (
        lax.psum_scatter(
            clip_up.astype(jnp.bfloat16), "client", scatter_dimension=0, tiled=True
        ).astype(jnp.float32),
        lax.psum_scatter(
            clip_down.astype(jnp.bfloat16), "client", scatter_dimension=1, tiled=True
        ).astype(jnp.float32),
    )
    client_count = lax.axis_size("client")
    region_count = lax.axis_size("region")
    count = client_count * region_count
    rows = D // count
    region_index = lax.axis_index("region")
    full_up, full_down = (
        lax.psum(summed_up.astype(jnp.bfloat16), "region").astype(jnp.float32),
        lax.psum(summed_down.astype(jnp.bfloat16), "region").astype(jnp.float32),
    )
    share_up = lax.dynamic_slice_in_dim(full_up, region_index * rows, rows, 0)
    share_down = lax.dynamic_slice_in_dim(full_down, region_index * rows, rows, 1)
    block = lax.axis_index("client") * region_count + region_index
    base_up = lax.dynamic_slice_in_dim(up_weight, block * rows, rows, 0).astype(jnp.float32)
    base_down = lax.dynamic_slice_in_dim(down_weight, block * rows, rows, 1).astype(jnp.float32)
    root = math.sqrt(count)
    scale = server_rate / (clip_rms * root)
    new_up = base_up + scale * (share_up + clip_rms * root * noise_up)
    new_down = base_down + scale * (share_down + clip_rms * root * noise_down)
    return (new_up, new_down)


MESH = pl.DeviceIdType.MESH
WIDE = 256


def dot(left, right):
    return jnp.dot(left, right, preferred_element_type=jnp.float32)


def dot_t(left, right):
    return lax.dot_general(
        left, right, (((1,), (1,)), ((), ())), preferred_element_type=jnp.float32
    )


def gelu_pair(pre):
    root = math.sqrt(2.0 / math.pi)
    square = pre * pre
    bent = jnp.tanh(root * (pre + 0.044715 * (square * pre)))
    half = 0.5 * (1.0 + bent)
    slope = half + 0.5 * pre * (1.0 - bent * bent) * (root * (1.0 + 0.134145 * square))
    return pre * half, slope


def round_kernel(
    sizes,
    hidden,
    goal,
    up_hbm,
    down_hbm,
    out_up,
    out_down,
    up,
    down,
    shares,
    goals,
    own_x,
    normed,
    resid0,
    resid1,
    acts,
    dpres,
    picked_n,
    picked_r,
    later_pre,
    total,
    sent,
    landed,
    squares,
    local_sems,
    in_s,
    in_r,
    sum_s,
    sum_r,
    z_s,
    z_r,
    y_s,
    y_r,
    core_s,
    core_r,
    tp_s,
    tp_r,
):
    n_tp, n_c, n_r = sizes
    bf16, f32 = jnp.bfloat16, jnp.float32
    tp, c, r = lax.axis_index("tp"), lax.axis_index("client"), lax.axis_index("region")
    tokens, width = own_x.shape[0] // STEPS, own_x.shape[1]
    local = up.shape[1]
    blocks = local // WIDE
    rows = tokens // n_tp
    both = STEPS * tokens
    part = width // 2
    core = lax.rem(tp, 2)
    core_peer = {"tp": tp + 1 - 2 * core}
    y_peer = {"region": 1 - r}
    me = r * n_c + c
    count = n_c * n_r
    block = c * n_r + r

    def remote(src, dst, send, recv, peer):
        return pltpu.make_async_remote_copy(
            src_ref=src, dst_ref=dst, send_sem=send, recv_sem=recv, device_id=peer,
            device_id_type=MESH,
        )

    def tp_peer(d):
        return lax.rem(tp + d, n_tp)

    def tp_from(d):
        return lax.rem(tp + n_tp - d, n_tp)

    def c_from(d):
        return lax.rem(c + n_c - d, n_c)

    load_up = pltpu.make_async_copy(up_hbm, up, local_sems.at[0])
    load_down = pltpu.make_async_copy(down_hbm, down, local_sems.at[1])
    load_up.start()
    load_down.start()

    barrier = pltpu.get_barrier_semaphore()
    for d in range(1, n_tp):
        pl.semaphore_signal(barrier, inc=1, device_id={"tp": tp_peer(d)}, device_id_type=MESH)
    for d in range(1, n_c):
        pl.semaphore_signal(
            barrier, inc=1, device_id={"client": lax.rem(c + d, n_c)}, device_id_type=MESH
        )
    pl.semaphore_signal(barrier, inc=1, device_id=y_peer, device_id_type=MESH)
    pl.semaphore_wait(barrier, n_tp + n_c - 1)

    pending = []

    def start(copy):
        copy.start()
        pending.append(copy)
        return copy

    for d in range(1, n_tp):
        start(remote(hidden, shares.at[tp], in_s.at[0, d], in_r.at[0, d], {"tp": tp_peer(d)}))
    for d in range(1, n_tp):
        to = pl.multiple_of(tp_peer(d) * rows, rows)
        start(
            remote(
                goal.at[:, pl.ds(to, rows), :], goals.at[tp], in_s.at[1, d], in_r.at[1, d],
                {"tp": tp_peer(d)},
            )
        )
    shares[tp] = hidden[...]
    mine = pl.multiple_of(tp * rows, rows)
    goals[tp] = goal[:, pl.ds(mine, rows), :]
    for d in range(1, n_tp):
        slot = shares.at[tp_from(d)]
        remote(slot, slot, in_s.at[0, d], in_r.at[0, d], {"tp": tp_from(d)}).wait_recv()
    xfloat = jnp.concatenate([shares[j].astype(f32) for j in range(n_tp)], axis=-1)
    xfloat = xfloat.reshape(STEPS * tokens, width)
    own_x[...] = xfloat.astype(bf16)
    normed[me] = (
        xfloat * lax.rsqrt(jnp.mean(xfloat * xfloat, axis=-1, keepdims=True) + 1e-06)
    ).astype(bf16)

    def half(ref, k, which):
        return ref.at[k, :, pl.ds(pl.multiple_of(which * part, part), part)]

    def z_start(ref, p):
        for d in range(1, n_c):
            block = half(ref, me, core)
            start(
                remote(
                    block, block, z_s.at[p, d], z_r.at[p, d], {"client": lax.rem(c + d, n_c)}
                )
            )
        block = half(ref, me, core)
        start(remote(block, block, y_s.at[p, 0], y_r.at[p, 0], y_peer))

    def z_end(ref, p):
        for d in range(1, n_c):
            k = r * n_c + c_from(d)
            block = half(ref, k, core)
            remote(
                block, block, z_s.at[p, d], z_r.at[p, d], {"client": c_from(d)}
            ).wait_recv()
            start(remote(block, block, y_s.at[p, d], y_r.at[p, d], y_peer))
            start(remote(block, block, core_s.at[p, d], core_r.at[p, d], core_peer))

    def y_end(ref, p):
        for d in range(n_c):
            k = (1 - r) * n_c + c_from(d)
            block = half(ref, k, core)
            remote(block, block, y_s.at[p, d], y_r.at[p, d], y_peer).wait_recv()
            start(remote(block, block, core_s.at[p, n_c + d], core_r.at[p, n_c + d], core_peer))

    def core_wait(ref, p, sources):
        for d in sources:
            k = (r if d < n_c else 1 - r) * n_c + c_from(d % n_c)
            block = half(ref, k, 1 - core)
            remote(block, block, core_s.at[p, d], core_r.at[p, d], core_peer).wait_recv()

    def core_end(ref, p):
        core_wait(ref, p, range(1, n_c))

    def other_end(ref, p):
        core_wait(ref, p, range(n_c, 2 * n_c))

    z_start(normed, 0)

    def columns(b):
        return pl.ds(pl.multiple_of(b * WIDE, WIDE), WIDE)

    total[...] = jnp.zeros_like(total)
    load_up.wait()
    load_down.wait()

    def first(b, unused):
        at = columns(b)
        pre = dot(normed[me], up[:, at])
        later_pre[:, at] = pre[tokens:]
        act, slope = gelu_pair(pre[:tokens])
        act = act.astype(bf16)
        acts[me, :tokens, at] = act
        dpres[me, :tokens, at] = slope.astype(bf16)
        total[...] += dot(act, down[at, :])
        return unused

    lax.fori_loop(0, blocks, first, 0)
    overlap_n = (local_rate * dot_t(normed[me, tokens:], normed[me, :tokens])).astype(bf16)

    for d in range(1, n_tp):
        slot = goals.at[tp_from(d)]
        remote(slot, slot, in_s.at[1, d], in_r.at[1, d], {"tp": tp_from(d)}).wait_recv()
    goal_rows = jnp.concatenate([goals[j].astype(f32) for j in range(n_tp)], axis=-1)

    def residual(step, ref):
        sent[step] = total[...].astype(bf16)
        for d in range(1, n_tp):
            to = pl.multiple_of(tp_peer(d) * rows, rows)
            start(
                remote(
                    sent.at[step, pl.ds(to, rows), :], landed.at[step, d - 1],
                    sum_s.at[2 * step, d], sum_r.at[2 * step, d], {"tp": tp_peer(d)},
                )
            )
        output = total[pl.ds(mine, rows), :]
        for d in range(1, n_tp):
            slot = landed.at[step, d - 1]
            remote(
                slot, slot, sum_s.at[2 * step, d], sum_r.at[2 * step, d], {"tp": tp_from(d)}
            ).wait_recv()
            output = output + landed[step, d - 1].astype(f32)
        held = own_x[pl.ds(pl.multiple_of(step * tokens + tp * rows, rows), rows), :]
        output = output + held.astype(f32)
        ref[me, pl.ds(mine, rows), :] = ((output - goal_rows[step]) / tokens).astype(bf16)
        for d in range(1, n_tp):
            slot = ref.at[me, pl.ds(mine, rows), :]
            start(
                remote(
                    slot, slot, sum_s.at[2 * step + 1, d], sum_r.at[2 * step + 1, d],
                    {"tp": tp_peer(d)},
                )
            )
        for d in range(1, n_tp):
            slot = ref.at[me, pl.ds(pl.multiple_of(tp_from(d) * rows, rows), rows), :]
            remote(
                slot, slot, sum_s.at[2 * step + 1, d], sum_r.at[2 * step + 1, d],
                {"tp": tp_from(d)},
            ).wait_recv()

    residual(0, resid0)
    z_start(resid0, 1)

    total[...] = jnp.zeros_like(total)

    def second(b, overlap_a):
        at = columns(b)
        back = dot_t(resid0[me], down[at, :])
        dpre = (back * dpres[me, :tokens, at].astype(f32)).astype(bf16)
        dpres[me, :tokens, at] = dpre
        act, slope = gelu_pair(later_pre[:, at] - dot(overlap_n, dpre))
        act = act.astype(bf16)
        acts[me, tokens:, at] = act
        dpres[me, tokens:, at] = slope.astype(bf16)
        total[...] += dot(act, down[at, :])
        return overlap_a + dot_t(act, acts[me, :tokens, at])

    overlap_a = lax.fori_loop(0, blocks, second, jnp.zeros((tokens, tokens), f32))
    total[...] -= dot((local_rate * overlap_a).astype(bf16), resid0[me])
    z_end(normed, 0)
    residual(1, resid1)
    z_start(resid1, 2)

    chosen = (
        lax.broadcasted_iota(jnp.int32, (WIDE, width), 1)
        == lax.broadcasted_iota(jnp.int32, (WIDE, width), 0) + block * (width // count)
    )
    chosen = jnp.where(chosen, 1.0, 0.0).astype(bf16)

    overlap_r = (local_rate * dot_t(resid1[me], resid0[me])).astype(bf16)

    def last(b, unused):
        at = columns(b)
        back = dot_t(resid1[me], down[at, :]) - dot(overlap_r, acts[me, :tokens, at])
        dpres[me, tokens:, at] = (back * dpres[me, tokens:, at].astype(f32)).astype(bf16)
        return unused

    lax.fori_loop(0, blocks, last, 0)
    rows_r = jnp.concatenate([resid0[me], resid1[me]], axis=0)
    products = dot_t(normed[me], normed[me]) * dot_t(dpres[me], dpres[me])
    products = products + dot_t(acts[me], acts[me]) * dot_t(rows_r, rows_r)
    squares[tp, me] = jnp.broadcast_to(jnp.sum(products, keepdims=True), squares.shape[2:])
    for d in range(1, n_c):
        slot = squares.at[tp, me]
        start(
            remote(slot, slot, z_s.at[3, d], z_r.at[3, d], {"client": lax.rem(c + d, n_c)})
        )
    slot = squares.at[tp, me]
    start(remote(slot, slot, y_s.at[3, 0], y_r.at[3, 0], y_peer))

    z_end(resid0, 1)
    y_end(normed, 0)
    core_end(normed, 0)
    core_end(resid0, 1)

    def stacked(ref, at):
        return ref[at].reshape(n_c * ref.shape[1], ref.shape[2])

    def early(start_slot, low, high):
        group = pl.ds(start_slot, n_c)
        overlaps = []
        for i in range(n_c):
            k = start_slot + i
            overlaps.append(
                (local_rate * dot_t(normed[k, tokens:], normed[k, :tokens])).astype(bf16)
            )

        def body(b, unused):
            at = columns(b)
            pre = dot(stacked(normed, group), up[:, at]).reshape(n_c, both, WIDE)
            back = dot_t(stacked(resid0, group), down[at, :]).reshape(n_c, tokens, WIDE)
            for i in range(n_c):
                k = start_slot + i
                act, slope = gelu_pair(pre[i, :tokens])
                acts[k, :tokens, at] = act.astype(bf16)
                dpre = (back[i] * slope).astype(bf16)
                dpres[k, :tokens, at] = dpre
                act, slope = gelu_pair(pre[i, tokens:] - dot(overlaps[i], dpre))
                acts[k, tokens:, at] = act.astype(bf16)
                dpres[k, tokens:, at] = slope.astype(bf16)
            return unused

        lax.fori_loop(low, high, body, 0)

    def pick(start_slot):
        group = pl.ds(start_slot, n_c)
        at = pl.ds(pl.multiple_of(start_slot * both, n_c * both), n_c * both)
        picked_n[:, at] = dot_t(chosen, stacked(normed, group)).astype(bf16)

    def late(start_slot):
        group = pl.ds(start_slot, n_c)
        overlaps = []
        for i in range(n_c):
            k = start_slot + i
            overlaps.append((local_rate * dot_t(resid1[k], resid0[k])).astype(bf16))

        def body(b, unused):
            at = columns(b)
            back = dot_t(stacked(resid1, group), down[at, :]).reshape(n_c, tokens, WIDE)
            for i in range(n_c):
                k = start_slot + i
                full = back[i] - dot(overlaps[i], acts[k, :tokens, at])
                dpres[k, tokens:, at] = (full * dpres[k, tokens:, at].astype(f32)).astype(bf16)
            return unused

        lax.fori_loop(0, blocks, body, 0)
        for turn, ref in enumerate((resid0, resid1)):
            rows_t = dot_t(chosen, stacked(ref, group)).astype(bf16)
            for i in range(n_c):
                to = (start_slot + i) * both + turn * tokens
                picked_r[:, pl.ds(pl.multiple_of(to, tokens), tokens)] = rows_t[
                    :, i * tokens : (i + 1) * tokens
                ]

    middle = blocks // 2 + 1
    early(r * n_c, 0, middle)
    y_end(resid0, 1)
    early(r * n_c, middle, blocks)
    pick(r * n_c)
    z_end(resid1, 2)
    for d in range(1, n_c):
        slot = squares.at[tp, r * n_c + c_from(d)]
        remote(slot, slot, z_s.at[3, d], z_r.at[3, d], {"client": c_from(d)}).wait_recv()
        start(remote(slot, slot, y_s.at[3, d], y_r.at[3, d], y_peer))
    other_end(normed, 0)
    other_end(resid0, 1)
    early((1 - r) * n_c, 0, middle)
    y_end(resid1, 2)
    early((1 - r) * n_c, middle, blocks)
    pick((1 - r) * n_c)
    for d in range(n_c):
        slot = squares.at[tp, (1 - r) * n_c + c_from(d)]
        remote(slot, slot, y_s.at[3, d], y_r.at[3, d], y_peer).wait_recv()
    for d in range(1, n_tp):
        slot = squares.at[tp]
        start(remote(slot, slot, tp_s.at[d], tp_r.at[d], {"tp": tp_peer(d)}))
    core_end(resid1, 2)
    late(r * n_c)
    other_end(resid1, 2)
    late((1 - r) * n_c)
    for d in range(1, n_tp):
        slot = squares.at[tp_from(d)]
        remote(slot, slot, tp_s.at[d], tp_r.at[d], {"tp": tp_from(d)}).wait_recv()

    bound = clip_rms * math.sqrt(2.0 * width * local * n_tp)
    factors = []
    for k in range(count):
        square = squares[0, k, :1]
        for t in range(1, n_tp):
            square = square + squares[t, k, :1]
        size = local_rate * jnp.sqrt(jnp.maximum(square, 0.0))
        factors.append(-local_rate * bound / jnp.maximum(size, bound))
    factor = jnp.concatenate(factors, axis=-1)
    picked_n[...] = (picked_n[...].astype(f32) * factor).astype(bf16)
    picked_r[...] = (picked_r[...].astype(f32) * factor).astype(bf16)

    def add(b, unused):
        at = columns(b)
        out_up[:, at] = dot(picked_n[...], dpres[:, :, at].reshape(count * both, WIDE))
        out_down[:, at] = dot(picked_r[...], acts[:, :, at].reshape(count * both, WIDE))
        return unused

    lax.fori_loop(0, blocks, add, 0)
    for copy in pending:
        copy.wait_send()


def gathered(sizes, hidden_in, target, up_weight, down_weight, noise_up, noise_down):
    n_tp, n_c, n_r = sizes
    count = n_c * n_r
    steps, tokens, share = hidden_in.shape[1:]
    width, local = up_weight.shape
    both = steps * tokens
    bf16, f32 = jnp.bfloat16, jnp.float32
    vmem = pl.BlockSpec(memory_space=pltpu.VMEM)
    dma = pltpu.SemaphoreType.DMA
    total_up, total_down = pl.pallas_call(
        functools.partial(round_kernel, sizes),
        out_shape=[jax.ShapeDtypeStruct((WIDE, local), f32)] * 2,
        in_specs=[vmem, vmem] + [pl.BlockSpec(memory_space=pl.ANY)] * 2,
        out_specs=[vmem, vmem],
        scratch_shapes=[
            pltpu.VMEM((width, local), bf16),
            pltpu.VMEM((local, width), bf16),
            pltpu.VMEM((n_tp, steps, tokens, share), bf16),
            pltpu.VMEM((n_tp, steps, tokens // n_tp, share), bf16),
            pltpu.VMEM((both, width), bf16),
            pltpu.VMEM((count, both, width), bf16),
            pltpu.VMEM((count, tokens, width), bf16),
            pltpu.VMEM((count, tokens, width), bf16),
            pltpu.VMEM((count, both, local), bf16),
            pltpu.VMEM((count, both, local), bf16),
            pltpu.VMEM((WIDE, count * both), bf16),
            pltpu.VMEM((WIDE, count * both), bf16),
            pltpu.VMEM((tokens, local), f32),
            pltpu.VMEM((tokens, width), f32),
            pltpu.VMEM((steps, tokens, width), bf16),
            pltpu.VMEM((steps, n_tp - 1, tokens // n_tp, width), bf16),
            pltpu.VMEM((n_tp, count, 8, both), f32),
            dma((2,)),
            dma((2, n_tp)),
            dma((2, n_tp)),
            dma((2 * steps, n_tp)),
            dma((2 * steps, n_tp)),
            dma((4, n_c)),
            dma((4, n_c)),
            dma((4, n_c)),
            dma((4, n_c)),
            dma((3, 2 * n_c)),
            dma((3, 2 * n_c)),
            dma((n_tp,)),
            dma((n_tp,)),
        ],
        compiler_params=pltpu.CompilerParams(
            collective_id=0, has_side_effects=True, vmem_limit_bytes=62 * 1024 * 1024
        ),
    )(hidden_in[0], target[0], up_weight, down_weight)

    rows = width // count
    block = lax.axis_index("client") * n_r + lax.axis_index("region")
    base_up = lax.dynamic_slice_in_dim(up_weight, block * rows, rows, 0).astype(f32)
    base_down = lax.dynamic_slice_in_dim(down_weight, block * rows, rows, 1).astype(f32)
    root = math.sqrt(count)
    scale = server_rate / (clip_rms * root)
    return (
        base_up + scale * (total_up[:rows] + clip_rms * root * noise_up),
        base_down + scale * (total_down[:rows].T + clip_rms * root * noise_down),
    )


def solution(mesh):
    sizes = tuple(mesh.shape[axis] for axis in ("tp", "client", "region"))
    few = sizes[1] * sizes[2] <= 8 and sizes[2] == 2 and sizes[0] % 2 == 0
    body = functools.partial(gathered, sizes) if few else shards
    placed = (
        P(("client", "region"), None, None, "tp"),
        P(("client", "region"), None, None, "tp"),
        P(None, "tp"),
        P("tp", None),
        P(("client", "region"), "tp"),
        P("tp", ("client", "region")),
    )
    return jax.shard_map(
        body,
        mesh=mesh,
        in_specs=placed,
        out_specs=(P(("client", "region"), "tp"), P("tp", ("client", "region"))),
        check_vma=False,
    )
```

```python
import functools
import math

import jax
import jax.numpy as jnp
from jax import lax
from jax.experimental import pallas as pl
from jax.experimental.pallas import tpu as pltpu
from jax.sharding import PartitionSpec as P

D = 1792
F = 7168
STEPS = 2


local_rate = 0.5
clip_rms = 0.08
server_rate = 0.02


def gelu_back(pre, back):
    return jax.vjp(lambda value: jax.nn.gelu(value, approximate=True), pre)[1](back)[0]


def contract_rows(left, right):
    return lax.dot_general(
        left, right, (((0,), (0,)), ((), ())), preferred_element_type=jnp.float32
    )


def shards(hidden_in, target, up_weight, down_weight, noise_up, noise_down):
    inputs_all, goals_all = (
        lax.all_gather(hidden_in, "tp", axis=3, tiled=True),
        lax.all_gather(target, "tp", axis=3, tiled=True),
    )
    inputs_all = inputs_all[0]
    goals_all = goals_all[0]
    w_up, w_down = (up_weight, down_weight)
    acc_up = jnp.zeros(up_weight.shape, jnp.float32)
    acc_down = jnp.zeros(down_weight.shape, jnp.float32)
    for turn in range(STEPS):
        inputs = inputs_all[turn]
        xfloat = inputs.astype(jnp.float32)
        normed = (
            xfloat * lax.rsqrt(jnp.mean(xfloat * xfloat, axis=-1, keepdims=True) + 1e-06)
        ).astype(jnp.bfloat16)
        pre = jnp.dot(normed, w_up, preferred_element_type=jnp.float32)
        act = jax.nn.gelu(pre, approximate=True).astype(jnp.bfloat16)
        partial_out = jnp.dot(act, w_down, preferred_element_type=jnp.float32)
        output = xfloat + lax.psum(partial_out.astype(jnp.bfloat16), "tp").astype(jnp.float32)
        resid = ((output - goals_all[turn].astype(jnp.float32)) / inputs.shape[0]).astype(
            jnp.bfloat16
        )
        grad_down = contract_rows(act, resid)
        back = lax.dot_general(
            resid, w_down, (((1,), (1,)), ((), ())), preferred_element_type=jnp.float32
        )
        dpre = gelu_back(pre, back).astype(jnp.bfloat16)
        grad_up = contract_rows(normed, dpre)
        acc_up = acc_up + grad_up
        acc_down = acc_down + grad_down
        if turn + 1 < STEPS:
            w_up = (w_up.astype(jnp.float32) - local_rate * grad_up).astype(jnp.bfloat16)
            w_down = (w_down.astype(jnp.float32) - local_rate * grad_down).astype(jnp.bfloat16)
    delta_up = -local_rate * acc_up
    delta_down = -local_rate * acc_down
    squared = lax.psum(jnp.sum(delta_up * delta_up) + jnp.sum(delta_down * delta_down), "tp")
    bound = clip_rms * math.sqrt(2.0 * D * F)
    factor = bound / jnp.maximum(jnp.sqrt(squared), bound)
    clip_up = lax.optimization_barrier((delta_up * factor).astype(jnp.bfloat16)).astype(jnp.float32)
    clip_down = lax.optimization_barrier((delta_down * factor).astype(jnp.bfloat16)).astype(
        jnp.float32
    )
    summed_up, summed_down = (
        lax.psum_scatter(
            clip_up.astype(jnp.bfloat16), "client", scatter_dimension=0, tiled=True
        ).astype(jnp.float32),
        lax.psum_scatter(
            clip_down.astype(jnp.bfloat16), "client", scatter_dimension=1, tiled=True
        ).astype(jnp.float32),
    )
    client_count = lax.axis_size("client")
    region_count = lax.axis_size("region")
    count = client_count * region_count
    rows = D // count
    region_index = lax.axis_index("region")
    full_up, full_down = (
        lax.psum(summed_up.astype(jnp.bfloat16), "region").astype(jnp.float32),
        lax.psum(summed_down.astype(jnp.bfloat16), "region").astype(jnp.float32),
    )
    share_up = lax.dynamic_slice_in_dim(full_up, region_index * rows, rows, 0)
    share_down = lax.dynamic_slice_in_dim(full_down, region_index * rows, rows, 1)
    block = lax.axis_index("client") * region_count + region_index
    base_up = lax.dynamic_slice_in_dim(up_weight, block * rows, rows, 0).astype(jnp.float32)
    base_down = lax.dynamic_slice_in_dim(down_weight, block * rows, rows, 1).astype(jnp.float32)
    root = math.sqrt(count)
    scale = server_rate / (clip_rms * root)
    new_up = base_up + scale * (share_up + clip_rms * root * noise_up)
    new_down = base_down + scale * (share_down + clip_rms * root * noise_down)
    return (new_up, new_down)


MESH = pl.DeviceIdType.MESH
WIDE = 256


def dot(left, right):
    return jnp.dot(left, right, preferred_element_type=jnp.float32)


def dot_t(left, right):
    return lax.dot_general(
        left, right, (((1,), (1,)), ((), ())), preferred_element_type=jnp.float32
    )


def gelu_pair(pre):
    root = math.sqrt(2.0 / math.pi)
    square = pre * pre
    bent = jnp.tanh(root * (pre + 0.044715 * (square * pre)))
    half = 0.5 * (1.0 + bent)
    slope = half + 0.5 * pre * (1.0 - bent * bent) * (root * (1.0 + 0.134145 * square))
    return pre * half, slope


def round_kernel(
    sizes,
    hidden,
    goal,
    up_hbm,
    down_hbm,
    out_up,
    out_down,
    up,
    down,
    shares,
    goals,
    own_x,
    normed,
    resid0,
    resid1,
    acts,
    dpres,
    picked_n,
    picked_r,
    later_pre,
    total,
    sent,
    landed,
    squares,
    local_sems,
    in_s,
    in_r,
    sum_s,
    sum_r,
    z_s,
    z_r,
    y_s,
    y_r,
    core_s,
    core_r,
    tp_s,
    tp_r,
):
    n_tp, n_c, n_r = sizes
    bf16, f32 = jnp.bfloat16, jnp.float32
    tp, c, r = lax.axis_index("tp"), lax.axis_index("client"), lax.axis_index("region")
    tokens, width = own_x.shape[0] // STEPS, own_x.shape[1]
    local = up.shape[1]
    blocks = local // WIDE
    rows = tokens // n_tp
    both = STEPS * tokens
    part = width // 2
    core = lax.rem(tp, 2)
    core_peer = {"tp": tp + 1 - 2 * core}
    y_peer = {"region": 1 - r}
    me = r * n_c + c
    count = n_c * n_r
    block = c * n_r + r

    def remote(src, dst, send, recv, peer):
        return pltpu.make_async_remote_copy(
            src_ref=src, dst_ref=dst, send_sem=send, recv_sem=recv, device_id=peer,
            device_id_type=MESH,
        )

    def tp_peer(d):
        return lax.rem(tp + d, n_tp)

    def tp_from(d):
        return lax.rem(tp + n_tp - d, n_tp)

    def c_from(d):
        return lax.rem(c + n_c - d, n_c)

    load_up = pltpu.make_async_copy(up_hbm, up, local_sems.at[0])
    load_down = pltpu.make_async_copy(down_hbm, down, local_sems.at[1])
    load_up.start()
    load_down.start()

    barrier = pltpu.get_barrier_semaphore()
    for d in range(1, n_tp):
        pl.semaphore_signal(barrier, inc=1, device_id={"tp": tp_peer(d)}, device_id_type=MESH)
    for d in range(1, n_c):
        pl.semaphore_signal(
            barrier, inc=1, device_id={"client": lax.rem(c + d, n_c)}, device_id_type=MESH
        )
    pl.semaphore_signal(barrier, inc=1, device_id=y_peer, device_id_type=MESH)
    pl.semaphore_wait(barrier, n_tp + n_c - 1)

    pending = []

    def start(copy):
        copy.start()
        pending.append(copy)
        return copy

    for d in range(1, n_tp):
        start(remote(hidden, shares.at[tp], in_s.at[0, d], in_r.at[0, d], {"tp": tp_peer(d)}))
    for d in range(1, n_tp):
        to = pl.multiple_of(tp_peer(d) * rows, rows)
        start(
            remote(
                goal.at[:, pl.ds(to, rows), :], goals.at[tp], in_s.at[1, d], in_r.at[1, d],
                {"tp": tp_peer(d)},
            )
        )
    shares[tp] = hidden[...]
    mine = pl.multiple_of(tp * rows, rows)
    goals[tp] = goal[:, pl.ds(mine, rows), :]
    for d in range(1, n_tp):
        slot = shares.at[tp_from(d)]
        remote(slot, slot, in_s.at[0, d], in_r.at[0, d], {"tp": tp_from(d)}).wait_recv()
    xfloat = jnp.concatenate([shares[j].astype(f32) for j in range(n_tp)], axis=-1)
    xfloat = xfloat.reshape(STEPS * tokens, width)
    own_x[...] = xfloat.astype(bf16)
    normed[me] = (
        xfloat * lax.rsqrt(jnp.mean(xfloat * xfloat, axis=-1, keepdims=True) + 1e-06)
    ).astype(bf16)

    def half(ref, k, which):
        return ref.at[k, :, pl.ds(pl.multiple_of(which * part, part), part)]

    def z_start(ref, p):
        for d in range(1, n_c):
            block = half(ref, me, core)
            start(
                remote(
                    block, block, z_s.at[p, d], z_r.at[p, d], {"client": lax.rem(c + d, n_c)}
                )
            )
        block = half(ref, me, core)
        start(remote(block, block, y_s.at[p, 0], y_r.at[p, 0], y_peer))

    def z_end(ref, p):
        for d in range(1, n_c):
            k = r * n_c + c_from(d)
            block = half(ref, k, core)
            remote(
                block, block, z_s.at[p, d], z_r.at[p, d], {"client": c_from(d)}
            ).wait_recv()
            start(remote(block, block, y_s.at[p, d], y_r.at[p, d], y_peer))
            start(remote(block, block, core_s.at[p, d], core_r.at[p, d], core_peer))

    def y_end(ref, p):
        for d in range(n_c):
            k = (1 - r) * n_c + c_from(d)
            block = half(ref, k, core)
            remote(block, block, y_s.at[p, d], y_r.at[p, d], y_peer).wait_recv()
            start(remote(block, block, core_s.at[p, n_c + d], core_r.at[p, n_c + d], core_peer))

    def core_wait(ref, p, sources):
        for d in sources:
            k = (r if d < n_c else 1 - r) * n_c + c_from(d % n_c)
            block = half(ref, k, 1 - core)
            remote(block, block, core_s.at[p, d], core_r.at[p, d], core_peer).wait_recv()

    def core_end(ref, p):
        core_wait(ref, p, range(1, n_c))

    def other_end(ref, p):
        core_wait(ref, p, range(n_c, 2 * n_c))

    z_start(normed, 0)

    def columns(b):
        return pl.ds(pl.multiple_of(b * WIDE, WIDE), WIDE)

    total[...] = jnp.zeros_like(total)
    load_up.wait()
    load_down.wait()

    def first(b, unused):
        at = columns(b)
        pre = dot(normed[me], up[:, at])
        later_pre[:, at] = pre[tokens:]
        act, slope = gelu_pair(pre[:tokens])
        act = act.astype(bf16)
        acts[me, :tokens, at] = act
        dpres[me, :tokens, at] = slope.astype(bf16)
        total[...] += dot(act, down[at, :])
        return unused

    lax.fori_loop(0, blocks, first, 0)
    overlap_n = (local_rate * dot_t(normed[me, tokens:], normed[me, :tokens])).astype(bf16)

    for d in range(1, n_tp):
        slot = goals.at[tp_from(d)]
        remote(slot, slot, in_s.at[1, d], in_r.at[1, d], {"tp": tp_from(d)}).wait_recv()
    goal_rows = jnp.concatenate([goals[j].astype(f32) for j in range(n_tp)], axis=-1)

    def residual(step, ref):
        sent[step] = total[...].astype(bf16)
        for d in range(1, n_tp):
            to = pl.multiple_of(tp_peer(d) * rows, rows)
            start(
                remote(
                    sent.at[step, pl.ds(to, rows), :], landed.at[step, d - 1],
                    sum_s.at[2 * step, d], sum_r.at[2 * step, d], {"tp": tp_peer(d)},
                )
            )
        output = total[pl.ds(mine, rows), :]
        for d in range(1, n_tp):
            slot = landed.at[step, d - 1]
            remote(
                slot, slot, sum_s.at[2 * step, d], sum_r.at[2 * step, d], {"tp": tp_from(d)}
            ).wait_recv()
            output = output + landed[step, d - 1].astype(f32)
        held = own_x[pl.ds(pl.multiple_of(step * tokens + tp * rows, rows), rows), :]
        output = output + held.astype(f32)
        ref[me, pl.ds(mine, rows), :] = ((output - goal_rows[step]) / tokens).astype(bf16)
        for d in range(1, n_tp):
            slot = ref.at[me, pl.ds(mine, rows), :]
            start(
                remote(
                    slot, slot, sum_s.at[2 * step + 1, d], sum_r.at[2 * step + 1, d],
                    {"tp": tp_peer(d)},
                )
            )
        for d in range(1, n_tp):
            slot = ref.at[me, pl.ds(pl.multiple_of(tp_from(d) * rows, rows), rows), :]
            remote(
                slot, slot, sum_s.at[2 * step + 1, d], sum_r.at[2 * step + 1, d],
                {"tp": tp_from(d)},
            ).wait_recv()

    residual(0, resid0)
    z_start(resid0, 1)

    total[...] = jnp.zeros_like(total)

    def second(b, overlap_a):
        at = columns(b)
        back = dot_t(resid0[me], down[at, :])
        dpre = (back * dpres[me, :tokens, at].astype(f32)).astype(bf16)
        dpres[me, :tokens, at] = dpre
        act, slope = gelu_pair(later_pre[:, at] - dot(overlap_n, dpre))
        act = act.astype(bf16)
        acts[me, tokens:, at] = act
        dpres[me, tokens:, at] = slope.astype(bf16)
        total[...] += dot(act, down[at, :])
        return overlap_a + dot_t(act, acts[me, :tokens, at])

    overlap_a = lax.fori_loop(0, blocks, second, jnp.zeros((tokens, tokens), f32))
    total[...] -= dot((local_rate * overlap_a).astype(bf16), resid0[me])
    z_end(normed, 0)
    residual(1, resid1)
    z_start(resid1, 2)

    chosen = (
        lax.broadcasted_iota(jnp.int32, (WIDE, width), 1)
        == lax.broadcasted_iota(jnp.int32, (WIDE, width), 0) + block * (width // count)
    )
    chosen = jnp.where(chosen, 1.0, 0.0).astype(bf16)

    overlap_r = (local_rate * dot_t(resid1[me], resid0[me])).astype(bf16)

    def last(b, unused):
        at = columns(b)
        back = dot_t(resid1[me], down[at, :]) - dot(overlap_r, acts[me, :tokens, at])
        dpres[me, tokens:, at] = (back * dpres[me, tokens:, at].astype(f32)).astype(bf16)
        return unused

    lax.fori_loop(0, blocks, last, 0)
    rows_r = jnp.concatenate([resid0[me], resid1[me]], axis=0)
    products = dot_t(normed[me], normed[me]) * dot_t(dpres[me], dpres[me])
    products = products + dot_t(acts[me], acts[me]) * dot_t(rows_r, rows_r)
    squares[tp, me] = jnp.broadcast_to(jnp.sum(products, keepdims=True), squares.shape[2:])
    for d in range(1, n_c):
        slot = squares.at[tp, me]
        start(
            remote(slot, slot, z_s.at[3, d], z_r.at[3, d], {"client": lax.rem(c + d, n_c)})
        )
    slot = squares.at[tp, me]
    start(remote(slot, slot, y_s.at[3, 0], y_r.at[3, 0], y_peer))

    z_end(resid0, 1)
    core_end(normed, 0)
    core_end(resid0, 1)

    def stacked(ref, at):
        return ref[at].reshape(n_c * ref.shape[1], ref.shape[2])

    def early(start_slot, low, high):
        group = pl.ds(start_slot, n_c)
        overlaps = []
        for i in range(n_c):
            k = start_slot + i
            overlaps.append(
                (local_rate * dot_t(normed[k, tokens:], normed[k, :tokens])).astype(bf16)
            )

        def body(b, unused):
            at = columns(b)
            pre = dot(stacked(normed, group), up[:, at]).reshape(n_c, both, WIDE)
            back = dot_t(stacked(resid0, group), down[at, :]).reshape(n_c, tokens, WIDE)
            for i in range(n_c):
                k = start_slot + i
                act, slope = gelu_pair(pre[i, :tokens])
                acts[k, :tokens, at] = act.astype(bf16)
                dpre = (back[i] * slope).astype(bf16)
                dpres[k, :tokens, at] = dpre
                act, slope = gelu_pair(pre[i, tokens:] - dot(overlaps[i], dpre))
                acts[k, tokens:, at] = act.astype(bf16)
                dpres[k, tokens:, at] = slope.astype(bf16)
            return unused

        lax.fori_loop(low, high, body, 0)

    def pick(start_slot):
        group = pl.ds(start_slot, n_c)
        at = pl.ds(pl.multiple_of(start_slot * both, n_c * both), n_c * both)
        picked_n[:, at] = dot_t(chosen, stacked(normed, group)).astype(bf16)

    def late(start_slot):
        group = pl.ds(start_slot, n_c)
        overlaps = []
        for i in range(n_c):
            k = start_slot + i
            overlaps.append((local_rate * dot_t(resid1[k], resid0[k])).astype(bf16))

        def body(b, unused):
            at = columns(b)
            back = dot_t(stacked(resid1, group), down[at, :]).reshape(n_c, tokens, WIDE)
            for i in range(n_c):
                k = start_slot + i
                full = back[i] - dot(overlaps[i], acts[k, :tokens, at])
                dpres[k, tokens:, at] = (full * dpres[k, tokens:, at].astype(f32)).astype(bf16)
            return unused

        lax.fori_loop(0, blocks, body, 0)
        for turn, ref in enumerate((resid0, resid1)):
            rows_t = dot_t(chosen, stacked(ref, group)).astype(bf16)
            for i in range(n_c):
                to = (start_slot + i) * both + turn * tokens
                picked_r[:, pl.ds(pl.multiple_of(to, tokens), tokens)] = rows_t[
                    :, i * tokens : (i + 1) * tokens
                ]

    middle = blocks // 2 + 1
    early(r * n_c, 0, middle)
    y_end(normed, 0)
    z_end(resid1, 2)
    early(r * n_c, middle, blocks)
    pick(r * n_c)
    y_end(resid0, 1)
    for d in range(1, n_c):
        slot = squares.at[tp, r * n_c + c_from(d)]
        remote(slot, slot, z_s.at[3, d], z_r.at[3, d], {"client": c_from(d)}).wait_recv()
        start(remote(slot, slot, y_s.at[3, d], y_r.at[3, d], y_peer))
    other_end(normed, 0)
    other_end(resid0, 1)
    early((1 - r) * n_c, 0, middle)
    y_end(resid1, 2)
    early((1 - r) * n_c, middle, blocks)
    pick((1 - r) * n_c)
    for d in range(n_c):
        slot = squares.at[tp, (1 - r) * n_c + c_from(d)]
        remote(slot, slot, y_s.at[3, d], y_r.at[3, d], y_peer).wait_recv()
    for d in range(1, n_tp):
        slot = squares.at[tp]
        start(remote(slot, slot, tp_s.at[d], tp_r.at[d], {"tp": tp_peer(d)}))
    core_end(resid1, 2)
    late(r * n_c)
    other_end(resid1, 2)
    late((1 - r) * n_c)
    for d in range(1, n_tp):
        slot = squares.at[tp_from(d)]
        remote(slot, slot, tp_s.at[d], tp_r.at[d], {"tp": tp_from(d)}).wait_recv()

    scale = server_rate / (clip_rms * math.sqrt(count))
    bound = clip_rms * math.sqrt(2.0 * width * local * n_tp)
    factors = []
    for k in range(count):
        square = squares[0, k, :1]
        for t in range(1, n_tp):
            square = square + squares[t, k, :1]
        size = local_rate * jnp.sqrt(jnp.maximum(square, 0.0))
        factors.append(-local_rate * bound / jnp.maximum(size, bound))
    factor = jnp.concatenate(factors, axis=-1)
    picked_n[...] = (picked_n[...].astype(f32) * factor).astype(bf16)
    picked_r[...] = (picked_r[...].astype(f32) * factor).astype(bf16)

    def add(b, unused):
        at = columns(b)
        summed = dot(picked_n[...], dpres[:, :, at].reshape(count * both, WIDE))
        out_up[:, at] = scale * summed + dot(chosen, up[:, at])
        summed = dot(picked_r[...], acts[:, :, at].reshape(count * both, WIDE))
        out_down[:, at] = scale * summed + dot_t(chosen, down[at, :])
        return unused

    lax.fori_loop(0, blocks, add, 0)
    for copy in pending:
        copy.wait_send()


def gathered(sizes, hidden_in, target, up_weight, down_weight, noise_up, noise_down):
    n_tp, n_c, n_r = sizes
    count = n_c * n_r
    steps, tokens, share = hidden_in.shape[1:]
    width, local = up_weight.shape
    both = steps * tokens
    bf16, f32 = jnp.bfloat16, jnp.float32
    vmem = pl.BlockSpec(memory_space=pltpu.VMEM)
    dma = pltpu.SemaphoreType.DMA
    total_up, total_down = pl.pallas_call(
        functools.partial(round_kernel, sizes),
        out_shape=[jax.ShapeDtypeStruct((WIDE, local), f32)] * 2,
        in_specs=[vmem, vmem] + [pl.BlockSpec(memory_space=pl.ANY)] * 2,
        out_specs=[vmem, vmem],
        scratch_shapes=[
            pltpu.VMEM((width, local), bf16),
            pltpu.VMEM((local, width), bf16),
            pltpu.VMEM((n_tp, steps, tokens, share), bf16),
            pltpu.VMEM((n_tp, steps, tokens // n_tp, share), bf16),
            pltpu.VMEM((both, width), bf16),
            pltpu.VMEM((count, both, width), bf16),
            pltpu.VMEM((count, tokens, width), bf16),
            pltpu.VMEM((count, tokens, width), bf16),
            pltpu.VMEM((count, both, local), bf16),
            pltpu.VMEM((count, both, local), bf16),
            pltpu.VMEM((WIDE, count * both), bf16),
            pltpu.VMEM((WIDE, count * both), bf16),
            pltpu.VMEM((tokens, local), f32),
            pltpu.VMEM((tokens, width), f32),
            pltpu.VMEM((steps, tokens, width), bf16),
            pltpu.VMEM((steps, n_tp - 1, tokens // n_tp, width), bf16),
            pltpu.VMEM((n_tp, count, 8, both), f32),
            dma((2,)),
            dma((2, n_tp)),
            dma((2, n_tp)),
            dma((2 * steps, n_tp)),
            dma((2 * steps, n_tp)),
            dma((4, n_c)),
            dma((4, n_c)),
            dma((4, n_c)),
            dma((4, n_c)),
            dma((3, 2 * n_c)),
            dma((3, 2 * n_c)),
            dma((n_tp,)),
            dma((n_tp,)),
        ],
        compiler_params=pltpu.CompilerParams(
            collective_id=0, has_side_effects=True, vmem_limit_bytes=62 * 1024 * 1024
        ),
    )(hidden_in[0], target[0], up_weight, down_weight)

    rows = width // count
    root = math.sqrt(count)
    scale = server_rate / (clip_rms * root)
    return (
        total_up[:rows] + scale * (clip_rms * root * noise_up),
        total_down[:rows].T + scale * (clip_rms * root * noise_down),
    )


def solution(mesh):
    sizes = tuple(mesh.shape[axis] for axis in ("tp", "client", "region"))
    few = sizes[1] * sizes[2] <= 8 and sizes[2] == 2 and sizes[0] % 2 == 0
    body = functools.partial(gathered, sizes) if few else shards
    placed = (
        P(("client", "region"), None, None, "tp"),
        P(("client", "region"), None, None, "tp"),
        P(None, "tp"),
        P("tp", None),
        P(("client", "region"), "tp"),
        P("tp", ("client", "region")),
    )
    return jax.shard_map(
        body,
        mesh=mesh,
        in_specs=placed,
        out_specs=(P(("client", "region"), "tp"), P("tp", ("client", "region"))),
        check_vma=False,
    )
```
